32 devices in a mesh: band: 16 (over z, y, core), fft: 2 (over x).
Axes of the slice: x: 2, y: 2, z: 4, core: 2. Of those that a mesh axis runs over, the one named last changes fastest.
Arguments:
- orbitals: float32 [32, 96, 9216], P('band', 'fft'), may hold values from -6 to 6
- owners: int32 [1], replicated, may hold values from 0 to 15
- cutoff_mask: int32 [96, 9216], P(None, 'fft'), may hold values from 0 to 1, as said below
Outputs:
- exchange_local: float32 [32, 96, 9216], P('band', 'fft')
- exchange_block: float32 [2, 96, 9216], P(None, 'fft')
The draws below stay inside these ranges and needn't reach their ends.
Inputs may be any that keep to these rules, and one draw needn't show every extreme that they name: cutoff_mask is 1 exactly at the frequencies whose squared length s(x)^2 + s(y)^2 + s(z)^2 lies between 1 and a cutoff, and 0 elsewhere (0 at frequency (0, 0, 0)); it is unchanged when the sign of any one frequency component is changed.
All inputs are finite; a program needn't handle non-finite values.
Results may differ from the reference program's by a relative error of at most 0.00029.
Values sent between devices are 32-bit elements; how exact they have to be, the bound alone decides.
No kernel may reach another device: no remote copies, remote signals or barrier semaphores. Data moves between devices by JAX's collectives and lax.ppermute only.
A program may use at most 128 MiB of HBM per device.

```python
import jax
import jax.numpy as jnp
from jax import lax

NG = 96
NLOC = 2
NBLK = 1
BANDS = 32
BLOCK_BANDS = 2
N_BAND = 16


def draw_cutoff_mask(key, part):
    positions = jnp.arange(NG, dtype=jnp.int32)
    signed = jnp.where(positions <= NG // 2, positions, positions - NG)
    squared = signed[:, None, None] * signed[:, None, None] + signed[None, :, None] * signed[None, :, None] + signed[None, None, :] * signed[None, None, :]
    radius_limit = jax.random.randint(key, (), NG * NG // 90, NG * NG // 6 + 1, dtype=jnp.int32)
    inside = (squared <= radius_limit) & (squared > 0)
    return inside.astype(jnp.int32).reshape(NG, NG * NG)


def level_of(rng, extent, cuts, low, largest):
    def one(position, parts):
        heights = jax.random.uniform(jax.random.fold_in(jax.random.fold_in(rng, 6), position), (parts,), jnp.float32, low / len(cuts), largest / len(cuts))
        return jnp.repeat(jnp.exp(heights), extent[position] // parts).reshape((-1,) + (1,) * (len(extent) - position - 1))

    factor_of = one(*cuts[0])
    for cut in cuts[1:]:
        factor_of = factor_of * one(*cut)
    return factor_of


def noise(stream_key, extent, deviation, reach, split=(), held_as=jnp.bfloat16):
    loudness = level_of(stream_key, extent, split, -0.22, 0.18) if split else 1.0
    result = jax.random.normal(stream_key, extent, jnp.float32) * deviation * loudness
    return jnp.minimum(jnp.maximum(result, -reach), reach).astype(held_as)


def setup_inputs(seed: int = 0) -> dict:
    key_list = jax.random.split(jax.random.key(seed), 4)
    orbitals = noise(key_list[0], (BANDS, NG, NG * NG), 1.0, 6.0, ((0, 16), (1, 2)), jnp.float32)
    owners = jax.random.randint(key_list[1], (NBLK,), 0, N_BAND).astype(jnp.int32)
    cutoff_mask = draw_cutoff_mask(jax.random.fold_in(key_list[3], 71), 0)
    return dict(orbitals=orbitals, owners=owners, cutoff_mask=cutoff_mask)


COULOMB = 400.0
EXCHANGE_MIX = 0.25


def make_kernel(cutoff_mask):
    positions = jnp.arange(NG, dtype=jnp.int32)
    signed = jnp.where(positions <= NG // 2, positions, positions - NG)
    squared = signed[:, None, None] * signed[:, None, None] + signed[None, :, None] * signed[None, :, None] + signed[None, None, :] * signed[None, None, :]
    weights = cutoff_mask.reshape(NG, NG, NG).astype(jnp.float32)
    return COULOMB * weights / jnp.maximum(squared, 1).astype(jnp.float32)


def reference(orbitals, owners, cutoff_mask):
    kernel = make_kernel(cutoff_mask)
    grid = orbitals.reshape(BANDS, NG, NG, NG)
    pieces = []
    for block_index in range(NBLK):
        start = (owners[block_index] * NLOC).astype(jnp.int32)
        pieces.append(lax.dynamic_slice_in_dim(grid, start, NLOC, 0))
    block_orbs = jnp.concatenate(pieces, axis=0)

    def per_band(carry, single):
        density = single[None] * block_orbs
        spectrum = jnp.fft.fftn(density, axes=(1, 2, 3)) * kernel
        potential = jnp.real(jnp.fft.ifftn(spectrum, axes=(1, 2, 3))).astype(jnp.float32)
        local_value = -EXCHANGE_MIX * jnp.sum(block_orbs * potential, axis=0)
        carry = carry - EXCHANGE_MIX * single[None] * potential
        return carry, local_value

    start_total = jnp.zeros((BLOCK_BANDS, NG, NG, NG), jnp.float32)
    block_total, local_values = lax.scan(per_band, start_total, grid)
    return local_values.reshape(BANDS, NG, NG * NG), block_total.reshape(BLOCK_BANDS, NG, NG * NG)
```

```python
import functools
import math

import jax
import jax.numpy as jnp
import numpy as np
from jax import lax
from jax.experimental import pallas as pl
from jax.experimental.pallas import tpu as pltpu
from jax.sharding import PartitionSpec as P

COULOMB = 400.0
EXCHANGE_MIX = 0.25


def broadcast(value, axis, source):
    kept = jnp.where(lax.axis_index(axis) == source, value, 0).astype(value.dtype)
    return lax.psum(kept, axis)


def dft_tables(count):
    positions = jnp.arange(count, dtype=jnp.int32)
    phases = positions[:, None] * positions[None, :] % count
    angles = phases.astype(jnp.float32) * (2.0 * math.pi / count)
    return (jnp.cos(angles), jnp.sin(angles))


def transform_dim(values, matrix, dim):
    source = "pabc"
    target = source[:dim] + "k" + source[dim + 1 :]
    pattern = source + "," + source[dim] + "k" + "->" + target
    return jnp.einsum(pattern, values, matrix, precision=lax.Precision.HIGHEST)


def forward_local(real_data, cosine, sine):
    casine = cosine + sine
    parts = [transform_dim(transform_dim(real_data, casine, 3), casine, 2)]
    stacked = jnp.stack(parts, axis=1)
    return stacked.reshape(stacked.shape[0], stacked.shape[1], stacked.shape[2], -1)


def spectral_middle(spectrum, kernel, cosine, sine):
    count_pairs, components, grid_size, flat_cells = spectrum.shape
    shaped = spectrum.reshape(count_pairs, components, grid_size, kernel.shape[1], grid_size)
    casine = cosine + sine
    scaled = transform_dim(shaped[:, 0], casine, 1) * kernel
    parts = [transform_dim(scaled, casine, 1)]
    return jnp.stack(parts, axis=1).reshape(count_pairs, components, grid_size, flat_cells)


def inverse_local(spectrum, cosine, sine):
    count_pairs, components, slab_rows, flat_cells = spectrum.shape
    grid_size = cosine.shape[0]
    shaped = spectrum.reshape(count_pairs, components, slab_rows, grid_size, grid_size)
    casine = cosine + sine
    result = transform_dim(transform_dim(shaped[:, 0], casine, 2), casine, 3)
    result = result / float(grid_size * grid_size * grid_size)
    return result.reshape(count_pairs, slab_rows, flat_cells)


def per_device_general(orbitals, owners, cutoff_mask):
    local_bands, slab_rows, flat_cells = orbitals.shape
    grid_size = slab_rows * lax.axis_size("fft")
    cosine, sine = dft_tables(grid_size)
    positions = jnp.arange(grid_size, dtype=jnp.int32)
    signed = jnp.where(positions <= grid_size // 2, positions, positions - grid_size)
    signed_y = lax.dynamic_slice_in_dim(signed, lax.axis_index("fft") * slab_rows, slab_rows)
    squared = (
        signed[:, None, None] * signed[:, None, None]
        + signed_y[None, :, None] * signed_y[None, :, None]
        + signed[None, None, :] * signed[None, None, :]
    )
    weights = cutoff_mask.reshape(grid_size, slab_rows, grid_size).astype(jnp.float32)
    kernel = COULOMB * weights / jnp.maximum(squared, 1).astype(jnp.float32)
    local_total = jnp.zeros((local_bands, slab_rows, flat_cells), jnp.float32)
    block_orbs = broadcast(orbitals, "band", owners[0])
    pair_data = (orbitals[:, None] * block_orbs[None]).reshape(
        local_bands * local_bands, slab_rows, grid_size, grid_size
    )
    spectrum = forward_local(pair_data, cosine, sine)
    pencil_out = spectral_middle(
        lax.all_to_all(spectrum, "fft", split_axis=3, concat_axis=2, tiled=True),
        kernel,
        cosine,
        sine,
    )
    returned = lax.all_to_all(pencil_out, "fft", split_axis=2, concat_axis=3, tiled=True)
    potential = inverse_local(returned, cosine, sine).reshape(
        local_bands, local_bands, slab_rows, flat_cells
    )
    local_total = local_total - EXCHANGE_MIX * jnp.sum(block_orbs[None] * potential, axis=1)
    block_terms = -EXCHANGE_MIX * jnp.sum(orbitals[:, None] * potential, axis=0)
    block_total = lax.psum(block_terms, "band")
    return (local_total, block_total)


LANES = 128


def casine_matrix(count):
    positions = np.arange(count)
    angles = (np.outer(positions, positions) % count) * (2.0 * np.pi / count)
    return np.cos(angles) + np.sin(angles)


def split_table(matrix):
    high = matrix.astype(np.float32).astype(jnp.bfloat16)
    low = (matrix - high.astype(np.float64)).astype(np.float32).astype(jnp.bfloat16)
    return high, low


def left_table(matrix):
    high, low = split_table(matrix)
    return np.concatenate([np.concatenate([high, high], 1), np.concatenate([low, low], 1)], 0)


def right_table(matrix):
    count = matrix.shape[0]
    padded = np.zeros((LANES, LANES))
    padded[:count, :count] = matrix
    row = np.concatenate(split_table(padded), 1)
    return np.concatenate([row, row], 0)


def split(values):
    high = values.astype(jnp.bfloat16)
    return high, (values - high.astype(jnp.float32)).astype(jnp.bfloat16)


def transform_rows(table, values):
    rows = values.shape[0]
    stacked = jnp.concatenate(split(values), 0)
    result = jnp.dot(table, stacked, preferred_element_type=jnp.float32)
    return result[:rows] + result[rows:]


def transform_lanes(values, table):
    stacked = jnp.concatenate(split(values), 1)
    result = jnp.dot(stacked, table, preferred_element_type=jnp.float32)
    return result[:, :LANES] + result[:, LANES:]


def pair_kernel(
    count, per_unit, has_total, own, other, block, coulomb, into_x, out_of_x, along_y, along_z, *rest
):
    total = rest[0] if has_total else None
    local_own, local_other, block_terms, cells = rest[-4:]
    half = count // 2
    unit = per_unit * count
    units = count // per_unit
    batch = next(k for k in (4, 3, 2, 1) if units % k == 0)
    planes = next(k for k in (16, 8, 4, 2, 1) if count % k == 0)
    width = batch * unit

    def forward(step, carry):
        columns = pl.ds(pl.multiple_of(step * width, LANES), width)
        density = jnp.concatenate([own[:, columns], other[:, columns]], 0) * block[:, columns]
        density = transform_rows(into_x[...], density)
        parts = []
        for start in range(0, width, unit):
            piece = density[:, start : start + unit]
            for index in range(per_unit):
                shifted = pltpu.roll(piece, unit - index * count, 1) if index else piece
                parts.append(shifted[:, :LANES])
        rows = pl.ds(pl.multiple_of(step * width, 8), width)
        cells[rows, :] = transform_lanes(jnp.concatenate(parts, 0), along_z[...])
        return carry

    lax.fori_loop(0, units // batch, forward, 0)

    def middle(step, carry):
        first = step * planes
        values = [cells[pl.ds(first + k, count, stride=count), :] for k in range(planes)]
        spectrum = transform_rows(along_y[...], jnp.concatenate(values, 1))
        scale = jnp.concatenate([coulomb[first + k] for k in range(planes)], 1)
        scaled = transform_rows(along_y[...], spectrum * scale)
        for k in range(planes):
            cells[pl.ds(first + k, count, stride=count), :] = scaled[:, k * LANES : (k + 1) * LANES]
        return carry

    lax.fori_loop(0, count // planes, middle, 0)
    lane = lax.broadcasted_iota(jnp.int32, (count, LANES), 1)

    def inverse(step, carry):
        rows = pl.ds(pl.multiple_of(step * width, 8), width)
        values = transform_lanes(cells[rows, :], along_z[...])
        tiles = [None] * (width // LANES)

        def add(tile, value):
            tiles[tile] = value if tiles[tile] is None else tiles[tile] + value

        for start in range(0, width, count):
            tile, offset = divmod(start, LANES)
            piece = values[start : start + count]
            if offset:
                piece = pltpu.roll(piece, offset, 1)
            if offset + count <= LANES:
                add(tile, piece)
            else:
                add(tile, jnp.where(lane >= offset, piece, 0.0))
                add(tile + 1, jnp.where(lane < offset, piece, 0.0))
        potential = transform_rows(out_of_x[...], jnp.concatenate(tiles, 1))
        columns = pl.ds(pl.multiple_of(step * width, LANES), width)
        local = block[:, columns] * potential
        terms = jnp.concatenate([own[:, columns], other[:, columns]], 0) * potential
        if has_total:
            terms = terms + total[:, columns]
        local_own[:, columns] = local[:half]
        local_other[:, columns] = local[half:]
        block_terms[:, columns] = terms
        return carry

    lax.fori_loop(0, units // batch, inverse, 0)


def pair_terms(own, other, block, coulomb, tables, total=None):
    half, flat_cells = own.shape
    count = 2 * half
    has_total = total is not None
    operands = [own, other, block, coulomb, *tables] + ([total] if has_total else [])
    vmem = pl.BlockSpec(memory_space=pltpu.VMEM)
    shapes = [(half, flat_cells), (half, flat_cells), (count, flat_cells)]
    return pl.pallas_call(
        functools.partial(pair_kernel, count, math.lcm(count, LANES) // count, has_total),
        in_specs=[vmem] * len(operands),
        out_specs=[vmem] * 3,
        out_shape=[jax.ShapeDtypeStruct(shape, jnp.float32) for shape in shapes],
        scratch_shapes=[pltpu.VMEM((flat_cells, LANES), jnp.float32)],
        compiler_params=pltpu.CompilerParams(vmem_limit_bytes=50 * 2**20),
        name="pair_terms",
    )(*operands)


def halves(values, upper, dim):
    size = values.shape[dim] // 2
    low = lax.slice_in_dim(values, 0, size, axis=dim)
    high = lax.slice_in_dim(values, size, 2 * size, axis=dim)
    return jnp.where(upper, high, low), jnp.where(upper, low, high)


def joined(mine, theirs, upper, dim):
    return jnp.concatenate(
        [jnp.where(upper, theirs, mine), jnp.where(upper, mine, theirs)], axis=dim
    )


def band_sum(values, exchange_x):
    size = lax.axis_size("band")
    index = lax.axis_index("band")
    core, side, depth = index % 2, index // 2 % 2, index // 4
    depth_low, depth_high = (depth + depth // 2) % 2 == 1, depth // 2 == 1

    def swap(value, partner):
        return lax.ppermute(value, "band", [(k, partner(k)) for k in range(size)])

    def by_core(first, second):
        return lambda k: k ^ (second if k % 2 else first)

    side_or_low = by_core(2, 4)
    low_or_high = by_core(4, 12)
    high_or_side = by_core(12, 2)
    first_bit = jnp.where(core == 1, depth_low, side == 1)
    second_bit = jnp.where(core == 1, depth_high, depth_low)
    keep, send = halves(values, core == 1, 1)
    values = keep + swap(send, lambda k: k ^ 1)
    keep, send = halves(values, first_bit, 2)
    values = keep + swap(send, side_or_low)
    keep, send = halves(values, second_bit, 2)
    values = keep + swap(send, low_or_high)
    values = values + swap(values, high_or_side)
    values = exchange_x(values)
    values = joined(values, swap(values, low_or_high), second_bit, 2)
    values = joined(values, swap(values, side_or_low), first_bit, 2)
    return joined(values, swap(values, lambda k: k ^ 1), core == 1, 1)


def across(value):
    return lax.ppermute(value, "fft", [(0, 1), (1, 0)])


def coulomb_table(cutoff_mask, count):
    columns = cutoff_mask.shape[1] // count
    positions = jnp.arange(count, dtype=jnp.int32)
    signed = jnp.where(positions <= count // 2, positions, positions - count)
    squares = signed * signed
    mine = lax.dynamic_slice_in_dim(squares, lax.axis_index("fft") * columns, columns)
    flat = (mine[:, None] + squares[None, :]).reshape(-1)
    lengths = jnp.where(cutoff_mask != 0, squares[:, None] + flat[None, :], 0)
    limit = jnp.full((8, LANES), jnp.max(lengths).astype(jnp.float32))
    limit = jnp.maximum(limit, across(limit))[0, 0].astype(jnp.int32)
    padded = jnp.concatenate([squares, jnp.full((LANES - count,), 4 * count * count, jnp.int32)])
    squared = squares[:, None, None] + squares[None, :, None] + padded[None, None, :]
    weights = ((squared >= 1) & (squared <= limit)).astype(jnp.float32)
    factor = -EXCHANGE_MIX * COULOMB / float(count**3)
    return factor * weights / jnp.maximum(squared, 1).astype(jnp.float32)


def per_device_pairs(orbitals, owners, cutoff_mask):
    _, half, flat_cells = orbitals.shape
    count = 2 * half
    plane = lax.axis_index("fft")
    casine = casine_matrix(count)
    turned = [(np.arange(count) + half * k) % count for k in range(2)]
    into_x = jnp.asarray(np.stack([left_table(casine[:, order]) for order in turned]))[plane]
    out_of_x = jnp.asarray(np.stack([left_table(casine[order, :]) for order in turned]))[plane]
    tables = [into_x, out_of_x, jnp.asarray(left_table(casine)), jnp.asarray(right_table(casine))]

    def gather_band(pieces):
        mine = jnp.where(plane == 1, pieces[1], pieces[0])
        theirs = jnp.where(plane == 1, pieces[0], pieces[1])
        return jnp.stack([mine, across(theirs)])

    def gather_half(pieces):
        other = across(pieces[1])
        return jnp.stack(
            [jnp.where(plane == 1, other, pieces[0]), jnp.where(plane == 1, pieces[0], other)]
        )

    first_other = across(orbitals[0])
    coulomb = coulomb_table(cutoff_mask, count)
    owned = jnp.where(lax.axis_index("band") == owners[0], orbitals, 0.0)
    block = band_sum(owned, gather_band).reshape(count, flat_cells)
    second, _ = lax.optimization_barrier((orbitals[1], first_other))
    second_other = across(second)
    own0, other0, terms = pair_terms(orbitals[0], first_other, block, coulomb, tables)
    own1, other1, terms = pair_terms(orbitals[1], second_other, block, coulomb, tables, terms)
    local_total = jnp.stack([own0 + across(other0), own1 + across(other1)])
    block_total = band_sum(terms.reshape(2, half, flat_cells), gather_half)
    return local_total, block_total


def solution(mesh):
    in_specs = (P("band", "fft", None), P(), P(None, "fft"))
    out_specs = (P("band", "fft", None), P(None, "fft", None))

    def per_device(orbitals, owners, cutoff_mask):
        bands, rows, cells = orbitals.shape
        paired = bands == mesh.shape["fft"] == 2 and mesh.shape["band"] == 16
        paired = paired and cells % (8 * LANES) == 0 and rows % 16 == 0 and 2 * rows <= LANES
        chosen = per_device_pairs if paired else per_device_general
        return chosen(orbitals, owners, cutoff_mask)

    return jax.shard_map(
        per_device, mesh=mesh, in_specs=in_specs, out_specs=out_specs, check_vma=False
    )
```

```python
import functools
import math

import jax
import jax.numpy as jnp
import numpy as np
from jax import lax
from jax.experimental import pallas as pl
from jax.experimental.pallas import tpu as pltpu
from jax.sharding import PartitionSpec as P

COULOMB = 400.0
EXCHANGE_MIX = 0.25


def broadcast(value, axis, source):
    kept = jnp.where(lax.axis_index(axis) == source, value, 0).astype(value.dtype)
    return lax.psum(kept, axis)


def dft_tables(count):
    positions = jnp.arange(count, dtype=jnp.int32)
    phases = positions[:, None] * positions[None, :] % count
    angles = phases.astype(jnp.float32) * (2.0 * math.pi / count)
    return (jnp.cos(angles), jnp.sin(angles))


def transform_dim(values, matrix, dim):
    source = "pabc"
    target = source[:dim] + "k" + source[dim + 1 :]
    pattern = source + "," + source[dim] + "k" + "->" + target
    return jnp.einsum(pattern, values, matrix, precision=lax.Precision.HIGHEST)


def forward_local(real_data, cosine, sine):
    casine = cosine + sine
    parts = [transform_dim(transform_dim(real_data, casine, 3), casine, 2)]
    stacked = jnp.stack(parts, axis=1)
    return stacked.reshape(stacked.shape[0], stacked.shape[1], stacked.shape[2], -1)


def spectral_middle(spectrum, kernel, cosine, sine):
    count_pairs, components, grid_size, flat_cells = spectrum.shape
    shaped = spectrum.reshape(count_pairs, components, grid_size, kernel.shape[1], grid_size)
    casine = cosine + sine
    scaled = transform_dim(shaped[:, 0], casine, 1) * kernel
    parts = [transform_dim(scaled, casine, 1)]
    return jnp.stack(parts, axis=1).reshape(count_pairs, components, grid_size, flat_cells)


def inverse_local(spectrum, cosine, sine):
    count_pairs, components, slab_rows, flat_cells = spectrum.shape
    grid_size = cosine.shape[0]
    shaped = spectrum.reshape(count_pairs, components, slab_rows, grid_size, grid_size)
    casine = cosine + sine
    result = transform_dim(transform_dim(shaped[:, 0], casine, 2), casine, 3)
    result = result / float(grid_size * grid_size * grid_size)
    return result.reshape(count_pairs, slab_rows, flat_cells)


def per_device_general(orbitals, owners, cutoff_mask):
    local_bands, slab_rows, flat_cells = orbitals.shape
    grid_size = slab_rows * lax.axis_size("fft")
    cosine, sine = dft_tables(grid_size)
    positions = jnp.arange(grid_size, dtype=jnp.int32)
    signed = jnp.where(positions <= grid_size // 2, positions, positions - grid_size)
    signed_y = lax.dynamic_slice_in_dim(signed, lax.axis_index("fft") * slab_rows, slab_rows)
    squared = (
        signed[:, None, None] * signed[:, None, None]
        + signed_y[None, :, None] * signed_y[None, :, None]
        + signed[None, None, :] * signed[None, None, :]
    )
    weights = cutoff_mask.reshape(grid_size, slab_rows, grid_size).astype(jnp.float32)
    kernel = COULOMB * weights / jnp.maximum(squared, 1).astype(jnp.float32)
    local_total = jnp.zeros((local_bands, slab_rows, flat_cells), jnp.float32)
    block_orbs = broadcast(orbitals, "band", owners[0])
    pair_data = (orbitals[:, None] * block_orbs[None]).reshape(
        local_bands * local_bands, slab_rows, grid_size, grid_size
    )
    spectrum = forward_local(pair_data, cosine, sine)
    pencil_out = spectral_middle(
        lax.all_to_all(spectrum, "fft", split_axis=3, concat_axis=2, tiled=True),
        kernel,
        cosine,
        sine,
    )
    returned = lax.all_to_all(pencil_out, "fft", split_axis=2, concat_axis=3, tiled=True)
    potential = inverse_local(returned, cosine, sine).reshape(
        local_bands, local_bands, slab_rows, flat_cells
    )
    local_total = local_total - EXCHANGE_MIX * jnp.sum(block_orbs[None] * potential, axis=1)
    block_terms = -EXCHANGE_MIX * jnp.sum(orbitals[:, None] * potential, axis=0)
    block_total = lax.psum(block_terms, "band")
    return (local_total, block_total)


LANES = 128


def casine_matrix(count):
    positions = np.arange(count)
    angles = (np.outer(positions, positions) % count) * (2.0 * np.pi / count)
    return np.cos(angles) + np.sin(angles)


def split_table(matrix):
    high = matrix.astype(np.float32).astype(jnp.bfloat16)
    low = (matrix - high.astype(np.float64)).astype(np.float32).astype(jnp.bfloat16)
    return high, low


def left_table(matrix):
    high, low = split_table(matrix)
    return np.concatenate([np.concatenate([high, high], 1), np.concatenate([low, low], 1)], 0)


def right_table(matrix):
    count = matrix.shape[0]
    padded = np.zeros((LANES, LANES))
    padded[:count, :count] = matrix
    row = np.concatenate(split_table(padded), 1)
    return np.concatenate([row, row], 0)


def split(values):
    high = values.astype(jnp.bfloat16)
    return high, (values - high.astype(jnp.float32)).astype(jnp.bfloat16)


def transform_rows(table, values):
    rows = values.shape[0]
    stacked = jnp.concatenate(split(values), 0)
    result = jnp.dot(table, stacked, preferred_element_type=jnp.float32)
    return result[:rows] + result[rows:]


def transform_lanes(values, table):
    stacked = jnp.concatenate(split(values), 1)
    result = jnp.dot(stacked, table, preferred_element_type=jnp.float32)
    return result[:, :LANES] + result[:, LANES:]


def divisor(total, limit):
    return max(k for k in range(1, limit + 1) if total % k == 0)


def pair_kernel(count, unit, batch, planes, band, has_total, sizes, core_ref, *refs):
    into_x, out_of_x, along_y, along_z, *refs = refs
    in_rows, out_rows = sizes
    half, quarter = count // 2, count // 4
    n_in = 6 + len(in_rows) + (4 if has_total else 0)
    n_out = 5 + len(out_rows)
    orbitals, coulomb_in, *others = refs[:n_in]
    block_in, totals_in, others = others[:4], others[4 + len(in_rows) :], others[4 : 4 + len(in_rows)]
    local_out, *backs = refs[n_in : n_in + n_out]
    terms_out, backs = backs[:4], backs[4:]
    first, second, coulomb, total, local, terms, cells, in_sems, out_sems, wide_sem = refs[n_in + n_out :]
    width = batch * unit
    steps = count * count // width
    mine, theirs = core_ref[0] * quarter, quarter - core_ref[0] * quarter

    def spans(buffer, pieces):
        result = []
        for ref, start, rows in pieces:
            start = start if isinstance(start, int) else pl.multiple_of(start, 8)
            result.append((ref, buffer.at[pl.ds(start, rows)]))
        return result

    def by_core(buffer, parts):
        starts = [k * half + start for k in range(2) for start in (mine, theirs)]
        return spans(buffer, [(ref, start, quarter) for ref, start in zip(parts, starts)])

    def by_size(buffer, own, rest, rows):
        starts = [half + sum(rows[:k]) for k in range(len(rows))]
        return spans(buffer, [(own, 0, half)] + list(zip(rest, starts, rows)))

    loads = by_size(first, orbitals.at[band], others, in_rows) + by_core(second, block_in)
    late = by_core(total, totals_in) if has_total else []
    stores = by_size(local, local_out, backs, out_rows) + by_core(terms, terms_out)

    def copies(pairs, sems, step, offset, outward):
        columns = pl.ds(pl.multiple_of(step * width, LANES), width)
        for k, (outside, inside) in enumerate(pairs):
            ends = (outside.at[:, columns], inside.at[:, columns])
            yield pltpu.make_async_copy(*(ends[::-1] if outward else ends), sems.at[offset + k, step])

    wide = pltpu.make_async_copy(coulomb_in, coulomb, wide_sem)
    for step in range(steps):
        for copy in copies(loads, in_sems, step, 0, False):
            copy.start()
    wide.start()
    for step in range(steps):
        for copy in copies(late, in_sems, step, len(loads), False):
            copy.start()

    def forward(step, carry):
        for copy in copies(loads, in_sems, step, 0, False):
            copy.wait()
        columns = pl.ds(pl.multiple_of(step * width, LANES), width)
        density = transform_rows(into_x[...], first[:, columns] * second[:, columns])
        parts = []
        for start in range(0, width, unit):
            piece = density[:, start : start + unit]
            for offset in range(0, unit, count):
                shifted = pltpu.roll(piece, unit - offset, 1) if offset else piece
                parts.append(shifted[:, :LANES])
        rows = pl.ds(pl.multiple_of(step * width, 8), width)
        cells[rows, :] = transform_lanes(jnp.concatenate(parts, 0), along_z[...])
        return carry

    lax.fori_loop(0, steps, forward, 0)
    wide.wait()

    def middle(step, carry):
        start = step * planes
        values = [cells[pl.ds(start + k, count, stride=count), :] for k in range(planes)]
        spectrum = transform_rows(along_y[...], jnp.concatenate(values, 1))
        scale = jnp.concatenate([coulomb[start + k] for k in range(planes)], 1)
        scaled = transform_rows(along_y[...], spectrum * scale)
        for k in range(planes):
            cells[pl.ds(start + k, count, stride=count), :] = scaled[:, k * LANES : (k + 1) * LANES]
        return carry

    lax.fori_loop(0, count // planes, middle, 0)
    lane = lax.broadcasted_iota(jnp.int32, (count, LANES), 1)

    def inverse(step, carry):
        rows = pl.ds(pl.multiple_of(step * width, 8), width)
        values = transform_lanes(cells[rows, :], along_z[...])
        tiles = [None] * (width // LANES)

        def add(tile, value):
            tiles[tile] = value if tiles[tile] is None else tiles[tile] + value

        for start in range(0, width, count):
            tile, offset = divmod(start, LANES)
            piece = values[start : start + count]
            if offset:
                piece = pltpu.roll(piece, offset, 1)
            if offset + count <= LANES:
                add(tile, piece)
            else:
                add(tile, jnp.where(lane >= offset, piece, 0.0))
                add(tile + 1, jnp.where(lane < offset, piece, 0.0))
        potential = transform_rows(out_of_x[...], jnp.concatenate(tiles, 1))
        for copy in copies(late, in_sems, step, len(loads), False):
            copy.wait()
        columns = pl.ds(pl.multiple_of(step * width, LANES), width)
        local[:, columns] = second[:, columns] * potential
        result = first[:, columns] * potential
        if has_total:
            result = result + total[:, columns]
        terms[:, columns] = result
        for copy in copies(stores, out_sems, step, 0, True):
            copy.start()
        return carry

    lax.fori_loop(0, steps, inverse, 0)
    for step in range(steps):
        for copy in copies(stores, out_sems, step, 0, True):
            copy.wait()


def pair_terms(orbitals, band, others, block, coulomb, core, tables, back_rows, totals=()):
    _, half, flat_cells = orbitals.shape
    count, quarter = 2 * half, half // 2
    unit = math.lcm(count, LANES)
    batch = divisor(flat_cells // unit, 8)
    planes = divisor(count, 16)
    steps = flat_cells // (batch * unit)
    in_rows, out_rows = tuple(v.shape[0] for v in others), tuple(back_rows)
    operands = [orbitals, coulomb, *block, *others, *totals]
    vmem = pl.BlockSpec(memory_space=pltpu.VMEM)
    anywhere = pl.BlockSpec(memory_space=pl.ANY)
    shapes = [(half, flat_cells)] + [(quarter, flat_cells)] * 4
    shapes += [(rows, flat_cells) for rows in out_rows]
    whole = pltpu.VMEM((count, flat_cells), jnp.float32)
    moved = 4 * sum(math.prod(s) for s in shapes + [v.shape for v in operands])
    sizes = (in_rows, out_rows)
    return pl.pallas_call(
        functools.partial(pair_kernel, count, unit, batch, planes, band, bool(totals), sizes),
        in_specs=[pl.BlockSpec(memory_space=pltpu.SMEM)]
        + [vmem] * len(tables)
        + [anywhere] * len(operands),
        out_specs=[anywhere] * len(shapes),
        out_shape=[jax.ShapeDtypeStruct(shape, jnp.float32) for shape in shapes],
        scratch_shapes=[
            whole,
            whole,
            pltpu.VMEM(coulomb.shape, jnp.float32),
            whole if totals else pltpu.VMEM((8, LANES), jnp.float32),
            whole,
            whole,
            pltpu.VMEM((flat_cells, LANES), jnp.float32),
            pltpu.SemaphoreType.DMA((9 + len(in_rows), steps)),
            pltpu.SemaphoreType.DMA((5 + len(out_rows), steps)),
            pltpu.SemaphoreType.DMA,
        ],
        compiler_params=pltpu.CompilerParams(vmem_limit_bytes=60 * 2**20),
        cost_estimate=pl.CostEstimate(
            flops=6 * flat_cells * count * 16 * LANES, bytes_accessed=moved, transcendentals=0
        ),
        name="pair_terms",
    )(core, *tables, *operands)


def halves(values, upper, dim):
    size = values.shape[dim] // 2
    low = lax.slice_in_dim(values, 0, size, axis=dim)
    high = lax.slice_in_dim(values, size, 2 * size, axis=dim)
    return jnp.where(upper, high, low), jnp.where(upper, low, high)


def joined(mine, theirs, upper, dim):
    return jnp.concatenate(
        [jnp.where(upper, theirs, mine), jnp.where(upper, mine, theirs)], axis=dim
    )


def across(value):
    return lax.ppermute(value, "fft", [(0, 1), (1, 0)])


def tied(*values):
    return lax.optimization_barrier(values)


def largest_length(cutoff_mask, count):
    columns = cutoff_mask.shape[1] // count
    positions = jnp.arange(count, dtype=jnp.int32)
    signed = jnp.where(positions <= count // 2, positions, positions - count)
    squares = signed * signed
    mine = lax.dynamic_slice_in_dim(squares, lax.axis_index("fft") * columns, columns)
    flat = (mine[:, None] + squares[None, :]).reshape(-1)
    lengths = jnp.where(cutoff_mask != 0, squares[:, None] + flat[None, :], 0)
    return jnp.full((8, LANES), jnp.max(lengths).astype(jnp.float32))


def coulomb_table(limit, count):
    positions = jnp.arange(count, dtype=jnp.int32)
    signed = jnp.where(positions <= count // 2, positions, positions - count)
    squares = signed * signed
    padded = jnp.concatenate([squares, jnp.full((LANES - count,), 4 * count * count, jnp.int32)])
    squared = squares[:, None, None] + squares[None, :, None] + padded[None, None, :]
    weights = ((squared >= 1) & (squared <= limit)).astype(jnp.float32)
    factor = -EXCHANGE_MIX * COULOMB / float(count**3)
    return factor * weights / jnp.maximum(squared, 1).astype(jnp.float32)


class Beside:
    def __init__(self, sends, needed=()):
        self.sends = sends
        self.needed = dict(needed)
        self.results = {}
        self.arrived = {}

    def open(self, step, *values):
        self.arrived[step] = None
        if step in self.sends:
            *values, send = tied(*values, self.sends[step])
            self.arrived[step] = across(send)
        return values

    def close(self, step, value):
        if step in self.sends:
            value, self.arrived[step] = tied(value, self.arrived[step])
        if step in self.needed:
            value, self.results[step] = tied(value, self.needed[step](self.results))
        return value

    def pieces(self, *steps):
        return [self.arrived[step] for step in steps]


def band_sum(parts, exchange, beside, flip):
    size, planes = lax.axis_size("band"), lax.axis_size("fft")
    index, plane = lax.axis_index("band"), lax.axis_index("fft")
    core, side, depth = index % 2, index // 2 % 2, index // 4
    depth_low, depth_high = (depth + depth // 2) % 2 == 1, depth // 2 == 1

    def swap(step, value, partner, kept=None):
        kept, value = beside.open(step, value if kept is None else kept, value)
        ends = [(k, f, partner(k, f)) for k in range(size) for f in range(planes)]
        pairs = [(k * planes + f, end * planes + f) for k, f, end in ends]
        arrived = lax.ppermute(value, ("band", "fft"), pairs)
        return kept, beside.close(step, arrived)

    def added(step, value, partner, kept=None):
        kept, arrived = swap(step, value, partner, kept)
        return kept + arrived

    def across_cores(k, f):
        return k ^ 1

    def axes(which, flipped):
        def by_core(first, second):
            return lambda k, f: k ^ (second if (k + which + flipped * f) % 2 else first)

        turned = (core + which + flipped * plane) % 2 == 1
        bits = jnp.where(turned, depth_low, side == 1), jnp.where(turned, depth_high, depth_low)
        return bits, (by_core(2, 4), by_core(4, 12), by_core(12, 2))

    def down(which):
        bits, partners = axes(which, flip)
        keep, send = parts[which]
        value = added((which, "core"), send, across_cores, keep)
        keep, send = halves(value, bits[0], 1)
        value = added((which, "first"), send, partners[0], keep)
        keep, send = halves(value, bits[1], 1)
        value = added((which, "second"), send, partners[1], keep)
        return added((which, "third"), value, partners[2])

    def up(which, value):
        bits, partners = axes(which, 0)
        value = joined(*swap((which, "up_second"), value, partners[1]), bits[1], 1)
        value = joined(*swap((which, "up_first"), value, partners[0]), bits[0], 1)
        return swap((which, "core_back"), value, across_cores)

    pieces = exchange(down(0), down(1))
    return [up(which, piece) for which, piece in enumerate(pieces)]


def per_device_pairs(orbitals, owners, cutoff_mask):
    _, half, flat_cells = orbitals.shape
    count = 2 * half
    plane = lax.axis_index("fft")
    core = lax.axis_index("band") % 2
    core_scalar = jnp.full((1,), core, jnp.int32)
    casine = casine_matrix(count)
    orders = [np.roll(np.arange(count), -half * k) for k in range(2)]
    into_x = jnp.asarray(np.stack([left_table(casine[:, order]) for order in orders]))[plane]
    out_of_x = jnp.asarray(np.stack([left_table(casine[order, :]) for order in orders]))[plane]
    along_y, along_z = jnp.asarray(left_table(casine)), jnp.asarray(right_table(casine))
    length = largest_length(cutoff_mask, count)

    def gather_band(first, second):
        mine, theirs = jnp.where(plane == 1, second, first), jnp.where(plane == 1, first, second)
        return mine, across(theirs)

    def gather_half(own, other):
        return own, across(other)

    sixth = half // 6
    cut = lambda band, start, rows: orbitals[band, sixth * start : sixth * (start + rows)]
    steps = [(0, "core")]
    steps += [(k, name) for name in ("first", "second", "third", "up_second") for k in range(2)]
    places = [(0, k) for k in range(6)] + [(1, k) for k in range(3)]
    beside = Beside(
        {step: cut(*place, 1) for step, place in zip(steps, places)},
        {
            (0, "first"): lambda got: (length, into_x, out_of_x),
            (0, "third"): lambda got: jnp.maximum(
                got[0, "first"][0], across(got[0, "first"][0])
            ),
            (1, "up_second"): lambda got: coulomb_table(
                got[0, "third"][0, 0].astype(jnp.int32), count
            ),
        },
    )
    owned = jnp.where(lax.axis_index("band") == owners[0], orbitals, 0.0)
    block = band_sum([halves(v, core == 1, 0) for v in owned], gather_band, beside, 1)
    tables = (*beside.results[0, "first"][1:], along_y, along_z)
    coulomb = beside.results[1, "up_second"]
    block = [*block[0], *block[1]]
    arrived = beside.pieces(*steps)
    block[0], last = tied(block[0], cut(1, 3, 3))
    last = across(last)
    own0, *rest = pair_terms(
        orbitals, 0, arrived[:6], block, coulomb, core_scalar, tables, [3 * sixth] + [sixth] * 3
    )
    terms, backs0 = rest[:4], rest[4:]
    back0 = across(backs0[0])
    own1, *rest = pair_terms(
        orbitals, 1, arrived[6:] + [last], block, coulomb, core_scalar, tables, [sixth] * 6, terms
    )
    terms, backs1 = rest[:4], rest[4:]
    *terms, back0 = tied(*terms, back0)
    beside = Beside(dict(zip(steps, backs0[1:] + backs1)))
    sums = band_sum([terms[:2], terms[2:]], gather_half, beside, 0)
    own_band, other_band = [joined(*parts, core == 1, 0) for parts in sums]
    block_total = jnp.stack(
        [jnp.where(plane == 1, other_band, own_band), jnp.where(plane == 1, own_band, other_band)]
    )
    arrived = beside.pieces(*steps)
    back0 = jnp.concatenate([back0] + arrived[:3], 0)
    back1 = jnp.concatenate(arrived[3:], 0)
    local_total = jnp.stack([own0 + back0, own1 + back1])
    return local_total, block_total


def solution(mesh):
    in_specs = (P("band", "fft", None), P(), P(None, "fft"))
    out_specs = (P("band", "fft", None), P(None, "fft", None))

    def per_device(orbitals, owners, cutoff_mask):
        bands, rows, cells = orbitals.shape
        paired = bands == mesh.shape["fft"] == 2 and mesh.shape["band"] == 16
        paired = paired and cells % (8 * LANES) == 0 and rows % 16 == 0 and 2 * rows <= LANES
        chosen = per_device_pairs if paired else per_device_general
        return chosen(orbitals, owners, cutoff_mask)

    return jax.shard_map(
        per_device, mesh=mesh, in_specs=in_specs, out_specs=out_specs, check_vma=False
    )
```

```python
import functools
import math

import jax
import jax.numpy as jnp
import numpy as np
from jax import lax
from jax.experimental import pallas as pl
from jax.experimental.pallas import tpu as pltpu
from jax.sharding import PartitionSpec as P

COULOMB = 400.0
EXCHANGE_MIX = 0.25


def broadcast(value, axis, source):
    kept = jnp.where(lax.axis_index(axis) == source, value, 0).astype(value.dtype)
    return lax.psum(kept, axis)


def dft_tables(count):
    positions = jnp.arange(count, dtype=jnp.int32)
    phases = positions[:, None] * positions[None, :] % count
    angles = phases.astype(jnp.float32) * (2.0 * math.pi / count)
    return (jnp.cos(angles), jnp.sin(angles))


def transform_dim(values, matrix, dim):
    source = "pabc"
    target = source[:dim] + "k" + source[dim + 1 :]
    pattern = source + "," + source[dim] + "k" + "->" + target
    return jnp.einsum(pattern, values, matrix, precision=lax.Precision.HIGHEST)


def forward_local(real_data, cosine, sine):
    casine = cosine + sine
    parts = [transform_dim(transform_dim(real_data, casine, 3), casine, 2)]
    stacked = jnp.stack(parts, axis=1)
    return stacked.reshape(stacked.shape[0], stacked.shape[1], stacked.shape[2], -1)


def spectral_middle(spectrum, kernel, cosine, sine):
    count_pairs, components, grid_size, flat_cells = spectrum.shape
    shaped = spectrum.reshape(count_pairs, components, grid_size, kernel.shape[1], grid_size)
    casine = cosine + sine
    scaled = transform_dim(shaped[:, 0], casine, 1) * kernel
    parts = [transform_dim(scaled, casine, 1)]
    return jnp.stack(parts, axis=1).reshape(count_pairs, components, grid_size, flat_cells)


def inverse_local(spectrum, cosine, sine):
    count_pairs, components, slab_rows, flat_cells = spectrum.shape
    grid_size = cosine.shape[0]
    shaped = spectrum.reshape(count_pairs, components, slab_rows, grid_size, grid_size)
    casine = cosine + sine
    result = transform_dim(transform_dim(shaped[:, 0], casine, 2), casine, 3)
    result = result / float(grid_size * grid_size * grid_size)
    return result.reshape(count_pairs, slab_rows, flat_cells)


def per_device_general(orbitals, owners, cutoff_mask):
    local_bands, slab_rows, flat_cells = orbitals.shape
    grid_size = slab_rows * lax.axis_size("fft")
    cosine, sine = dft_tables(grid_size)
    positions = jnp.arange(grid_size, dtype=jnp.int32)
    signed = jnp.where(positions <= grid_size // 2, positions, positions - grid_size)
    signed_y = lax.dynamic_slice_in_dim(signed, lax.axis_index("fft") * slab_rows, slab_rows)
    squared = (
        signed[:, None, None] * signed[:, None, None]
        + signed_y[None, :, None] * signed_y[None, :, None]
        + signed[None, None, :] * signed[None, None, :]
    )
    weights = cutoff_mask.reshape(grid_size, slab_rows, grid_size).astype(jnp.float32)
    kernel = COULOMB * weights / jnp.maximum(squared, 1).astype(jnp.float32)
    local_total = jnp.zeros((local_bands, slab_rows, flat_cells), jnp.float32)
    block_orbs = broadcast(orbitals, "band", owners[0])
    pair_data = (orbitals[:, None] * block_orbs[None]).reshape(
        local_bands * local_bands, slab_rows, grid_size, grid_size
    )
    spectrum = forward_local(pair_data, cosine, sine)
    pencil_out = spectral_middle(
        lax.all_to_all(spectrum, "fft", split_axis=3, concat_axis=2, tiled=True),
        kernel,
        cosine,
        sine,
    )
    returned = lax.all_to_all(pencil_out, "fft", split_axis=2, concat_axis=3, tiled=True)
    potential = inverse_local(returned, cosine, sine).reshape(
        local_bands, local_bands, slab_rows, flat_cells
    )
    local_total = local_total - EXCHANGE_MIX * jnp.sum(block_orbs[None] * potential, axis=1)
    block_terms = -EXCHANGE_MIX * jnp.sum(orbitals[:, None] * potential, axis=0)
    block_total = lax.psum(block_terms, "band")
    return (local_total, block_total)


LANES = 128


def casine_matrix(count):
    positions = np.arange(count)
    angles = (np.outer(positions, positions) % count) * (2.0 * np.pi / count)
    return np.cos(angles) + np.sin(angles)


def split_table(matrix):
    high = matrix.astype(np.float32).astype(jnp.bfloat16)
    low = (matrix - high.astype(np.float64)).astype(np.float32).astype(jnp.bfloat16)
    return high, low


def left_table(matrix):
    high, low = split_table(matrix)
    return np.concatenate([np.concatenate([high, high], 1), np.concatenate([low, low], 1)], 0)


def right_table(matrix):
    count = matrix.shape[0]
    padded = np.zeros((LANES, LANES))
    padded[:count, :count] = matrix
    row = np.concatenate(split_table(padded), 1)
    return np.concatenate([row, row], 0)


def split(values):
    high = values.astype(jnp.bfloat16)
    return high, (values - high.astype(jnp.float32)).astype(jnp.bfloat16)


def transform_rows(table, values):
    rows = values.shape[0]
    stacked = jnp.concatenate(split(values), 0)
    result = jnp.dot(table, stacked, preferred_element_type=jnp.float32)
    return result[:rows] + result[rows:]


def transform_lanes(values, table):
    stacked = jnp.concatenate(split(values), 1)
    result = jnp.dot(stacked, table, preferred_element_type=jnp.float32)
    return result[:, :LANES] + result[:, LANES:]


def divisor(total, limit):
    return max(k for k in range(1, limit + 1) if total % k == 0)


def pair_kernel(count, unit, batch, planes, specs, has_total, place_ref, *refs):
    in_specs, out_specs = specs
    forth, along_z, *refs = refs
    half, quarter = count // 2, count // 4
    n_in = 5 + len(in_specs) + (4 if has_total else 0)
    n_out = 4 + len(out_specs)
    coulomb_in, *others = refs[:n_in]
    block_in, orbital_in, totals_in = others[:4], others[4 : 4 + len(in_specs)], others[4 + len(in_specs) :]
    terms_out, local_out = refs[n_in : n_in + 4], refs[n_in + 4 : n_in + n_out]
    first, second, coulomb, total, local, terms, cells, in_sems, out_sems, wide_sem = refs[n_in + n_out :]
    width = batch * unit
    steps = count * count // width
    plane, core = place_ref[0], place_ref[1]
    starts = (plane * half, half - plane * half)
    parts = (core * quarter, quarter - core * quarter)

    def span(ref, buffer, start, rows):
        start = start if isinstance(start, int) else pl.multiple_of(start, 8)
        return ref, buffer.at[pl.ds(start, rows)]

    def by_core(buffer, arrays):
        places = [start + part for start in starts for part in parts]
        return [span(ref, buffer, start, quarter) for ref, start in zip(arrays, places)]

    def by_spec(buffer, arrays, given):
        result = []
        for ref, (index, which, row, rows) in zip(arrays, given):
            ref = ref if index is None else ref.at[index]
            if which is None:
                result += [span(ref.at[k], buffer, k * half, half) for k in range(2)]
            else:
                result.append(span(ref, buffer, starts[which] + row, rows))
        return result

    loads = by_spec(first, orbital_in, in_specs) + by_core(second, block_in)
    late = by_core(total, totals_in) if has_total else []
    stores = by_core(terms, terms_out) + by_spec(local, local_out, out_specs)

    def copies(pairs, sems, step, offset, outward):
        columns = pl.ds(pl.multiple_of(step * width, LANES), width)
        for k, (outside, inside) in enumerate(pairs):
            ends = (outside.at[:, columns], inside.at[:, columns])
            yield pltpu.make_async_copy(*(ends[::-1] if outward else ends), sems.at[offset + k, step])

    wide = pltpu.make_async_copy(coulomb_in, coulomb, wide_sem)
    for step in range(steps):
        for copy in copies(loads, in_sems, step, 0, False):
            copy.start()
    wide.start()

    def forward(step, carry):
        for copy in copies(loads, in_sems, step, 0, False):
            copy.wait()
        columns = pl.ds(pl.multiple_of(step * width, LANES), width)
        density = transform_rows(forth[...], first[:, columns] * second[:, columns])
        pieces = []
        for start in range(0, width, unit):
            piece = density[:, start : start + unit]
            for offset in range(0, unit, count):
                shifted = pltpu.roll(piece, unit - offset, 1) if offset else piece
                pieces.append(shifted[:, :LANES])
        rows = pl.ds(pl.multiple_of(step * width, 8), width)
        cells[pl.ds(step * (width // count), width // count)] = transform_lanes(jnp.concatenate(pieces, 0), along_z[...]).reshape(width // count, count, LANES)
        return carry

    lax.fori_loop(0, steps, forward, 0)
    for step in range(steps):
        for copy in copies(late, in_sems, step, len(loads), False):
            copy.start()
    wide.wait()

    def middle(step, carry):
        start = step * planes
        cube = jnp.swapaxes(cells[:, pl.ds(pl.multiple_of(start, 8), planes), :], 0, 1)
        values = [cube[k] for k in range(planes)]
        spectrum = transform_rows(forth[...], jnp.concatenate(values, 1))
        scale = jnp.concatenate([coulomb[start + k] for k in range(planes)], 1)
        scaled = transform_rows(forth[...], spectrum * scale)
        cube = jnp.stack([scaled[:, k * LANES : (k + 1) * LANES] for k in range(planes)], 0)
        cells[:, pl.ds(pl.multiple_of(start, 8), planes), :] = jnp.swapaxes(cube, 0, 1)
        return carry

    lax.fori_loop(0, count // planes, middle, 0)
    lane = lax.broadcasted_iota(jnp.int32, (count, LANES), 1)

    def inverse(step, carry):
        rows = pl.ds(pl.multiple_of(step * width, 8), width)
        values = transform_lanes(cells[pl.ds(step * (width // count), width // count)].reshape(width, LANES), along_z[...])
        tiles = [None] * (width // LANES)

        def add(tile, value):
            tiles[tile] = value if tiles[tile] is None else tiles[tile] + value

        for start in range(0, width, count):
            tile, offset = divmod(start, LANES)
            piece = values[start : start + count]
            if offset:
                piece = pltpu.roll(piece, offset, 1)
            if offset + count <= LANES:
                add(tile, piece)
            else:
                add(tile, jnp.where(lane >= offset, piece, 0.0))
                add(tile + 1, jnp.where(lane < offset, piece, 0.0))
        potential = transform_rows(forth[...], jnp.concatenate(tiles, 1))
        for copy in copies(late, in_sems, step, len(loads), False):
            copy.wait()
        columns = pl.ds(pl.multiple_of(step * width, LANES), width)
        local[:, columns] = second[:, columns] * potential
        result = first[:, columns] * potential
        if has_total:
            result = result + total[:, columns]
        terms[:, columns] = result
        for copy in copies(stores, out_sems, step, 0, True):
            copy.start()
        return carry

    lax.fori_loop(0, steps, inverse, 0)
    for step in range(steps):
        for copy in copies(stores, out_sems, step, 0, True):
            copy.wait()


def pair_terms(orbital, block, coulomb, place, tables, out_specs, totals=()):
    arrays, in_specs = zip(*orbital)
    quarter, flat_cells = block[0].shape
    count = 4 * quarter
    unit = math.lcm(count, LANES)
    batch = divisor(flat_cells // unit, 12)
    planes = divisor(count, 16)
    steps = flat_cells // (batch * unit)
    operands = [coulomb, *block, *arrays, *totals]
    vmem = pl.BlockSpec(memory_space=pltpu.VMEM)
    anywhere = pl.BlockSpec(memory_space=pl.ANY)
    shapes = [(quarter, flat_cells)] * 4
    for _, which, _, rows in out_specs:
        shapes.append((2, 2 * quarter, flat_cells) if which is None else (rows, flat_cells))
    whole = pltpu.VMEM((count, flat_cells), jnp.float32)
    moved = 4 * sum(math.prod(s) for s in shapes + [v.shape for v in operands])
    specs = (tuple(in_specs), tuple(out_specs))
    return pl.pallas_call(
        functools.partial(pair_kernel, count, unit, batch, planes, specs, bool(totals)),
        in_specs=[pl.BlockSpec(memory_space=pltpu.SMEM)]
        + [vmem] * len(tables)
        + [anywhere] * len(operands),
        out_specs=[anywhere] * len(shapes),
        out_shape=[jax.ShapeDtypeStruct(shape, jnp.float32) for shape in shapes],
        scratch_shapes=[
            whole,
            whole,
            pltpu.VMEM(coulomb.shape, jnp.float32),
            whole if totals else pltpu.VMEM((8, LANES), jnp.float32),
            whole,
            whole,
            pltpu.VMEM((count, count, LANES), jnp.float32),
            pltpu.SemaphoreType.DMA((10 + len(in_specs), steps)),
            pltpu.SemaphoreType.DMA((6 + len(out_specs), steps)),
            pltpu.SemaphoreType.DMA,
        ],
        compiler_params=pltpu.CompilerParams(vmem_limit_bytes=60 * 2**20),
        cost_estimate=pl.CostEstimate(
            flops=6 * flat_cells * count * 16 * LANES, bytes_accessed=moved, transcendentals=0
        ),
        name="pair_terms",
    )(place, *tables, *operands)


def halves(values, upper, dim):
    size = values.shape[dim] // 2
    low = lax.slice_in_dim(values, 0, size, axis=dim)
    high = lax.slice_in_dim(values, size, 2 * size, axis=dim)
    return jnp.where(upper, high, low), jnp.where(upper, low, high)


def joined(mine, theirs, upper, dim):
    return jnp.concatenate(
        [jnp.where(upper, theirs, mine), jnp.where(upper, mine, theirs)], axis=dim
    )


def across(value):
    return lax.ppermute(value, "fft", [(0, 1), (1, 0)])


def tied(*values):
    return lax.optimization_barrier(values)


def squared_components(count):
    positions = np.arange(count)
    return np.where(positions <= count // 2, positions, positions - count).astype(np.int32) ** 2


def largest_length(cutoff_mask, count):
    squares = squared_components(count)
    flat = (squares[:, None] + squares[None, :]).reshape(-1, cutoff_mask.shape[1])
    mine = jnp.asarray(flat)[lax.axis_index("fft")]
    lengths = jnp.where(cutoff_mask != 0, squares[:, None] + mine[None, :], 0)
    return jnp.full((8, LANES), jnp.max(lengths).astype(jnp.float32))


def coulomb_table(limit, count):
    def squares(dim):
        position = lax.broadcasted_iota(jnp.int32, (count, count, LANES), dim)
        signed = jnp.where(position <= count // 2, position, position - count)
        return signed * signed

    squared = squares(0) + squares(1) + squares(2)
    weights = ((squared >= 1) & (squared <= limit)).astype(jnp.float32)
    factor = -EXCHANGE_MIX * COULOMB / float(count**3)
    return factor * weights / jnp.maximum(squared, 1).astype(jnp.float32)


def rows_of(array, index, start, rows):
    return array[index, start : start + rows]


class Beside:
    def __init__(self, sends, needed=()):
        self.sends = sends
        self.needed = dict(needed)
        self.results = {}
        self.arrived = {}

    def open(self, step, *values):
        if step in self.sends:
            array, *cut = self.sends[step]
            *values, array = tied(*values, array)
            self.arrived[step] = across(rows_of(array, *cut))
        if step in self.needed:
            array, function = self.needed[step]
            *values, array = tied(*values, array)
            self.results[step] = function(array, self.results)
        return values

    def close(self, step, value):
        for found in (self.arrived, self.results):
            if step in found:
                value, found[step] = tied(value, found[step])
        return value


def band_sum(parts, exchange, beside, flip):
    size, planes = lax.axis_size("band"), lax.axis_size("fft")
    index, plane = lax.axis_index("band"), lax.axis_index("fft")
    core, side, depth = index % 2, index // 2 % 2, index // 4
    depth_low, depth_high = (depth + depth // 2) % 2 == 1, depth // 2 == 1

    def swap(step, value, partner, kept=None):
        kept, value = beside.open(step, value if kept is None else kept, value)
        ends = [(k, f, partner(k, f)) for k in range(size) for f in range(planes)]
        pairs = [(k * planes + f, end * planes + f) for k, f, end in ends]
        arrived = lax.ppermute(value, ("band", "fft"), pairs)
        return kept, beside.close(step, arrived)

    def added(step, value, partner, kept=None):
        kept, arrived = swap(step, value, partner, kept)
        return kept + arrived

    def across_cores(k, f):
        return k ^ 1

    def axes(which, flipped):
        def by_core(first, second):
            return lambda k, f: k ^ (second if (k + which + flipped * f) % 2 else first)

        turned = (core + which + flipped * plane) % 2 == 1
        bits = jnp.where(turned, depth_low, side == 1), jnp.where(turned, depth_high, depth_low)
        return bits, (by_core(2, 4), by_core(4, 12), by_core(12, 2))

    def after(value, other):
        return value

    values = [None, None]
    earlier = [None, None]
    for which, (keep, send) in enumerate(parts):
        values[which] = added((which, "core"), send, across_cores, keep)
    for number, name in enumerate(("first", "second", "third")):
        results = []
        for which in range(2):
            bits, partners = axes(which, flip)
            value = after(values[which], earlier[1 - which])
            if number < 2:
                keep, send = halves(value, bits[number], 1)
                results.append(added((which, name), send, partners[number], keep))
            else:
                results.append(added((which, name), value, partners[number]))
        earlier, values = values, results
    values = exchange(*values)
    earlier = [None, None]
    for number, name in ((1, "up_second"), (0, "up_first")):
        results = []
        for which in range(2):
            bits, partners = axes(which, 0)
            value = after(values[which], earlier[1 - which])
            results.append(joined(*swap((which, name), value, partners[number]), bits[number], 1))
        earlier, values = values, results
    return [
        swap((which, "core_back"), after(values[which], earlier[1 - which]), across_cores)
        for which in range(2)
    ]


def per_device_pairs(orbitals, owners, cutoff_mask):
    _, half, flat_cells = orbitals.shape
    count = 2 * half
    plane = lax.axis_index("fft")
    core = lax.axis_index("band") % 2
    place = jnp.stack([plane, core]).astype(jnp.int32)
    casine = casine_matrix(count)
    tables = (jnp.asarray(left_table(casine)), jnp.asarray(right_table(casine)))
    sixth = half // 6

    def gather_band(first, second):
        mine, theirs = jnp.where(plane == 1, second, first), jnp.where(plane == 1, first, second)
        return mine, across(theirs)

    def gather_half(own, other):
        return own, across(other)

    def pieces(sizes):
        return [(None, 1, sixth * sum(sizes[:k]), sixth * size) for k, size in enumerate(sizes)]

    def sent(names, band, sizes):
        rows = pieces(sizes)
        return {(1, name): (orbitals, band, *spec[2:]) for name, spec in zip(names, rows)}

    steps = ("first", "second", "third", "up_second", "up_first")
    names = [(k, name) for name in steps for k in range(2)]
    sizes = ((1,) * 6, (1, 1, 1, 1, 2))
    rows = [(orbitals, band, *spec[2:]) for band in range(2) for spec in pieces(sizes[band])]
    beside = Beside(
        dict(zip(names, rows)),
        {
            (0, "first"): (cutoff_mask, lambda mask, got: largest_length(mask, count)),
            (0, "second"): (
                cutoff_mask,
                lambda _, got: jnp.maximum(got[0, "first"], across(got[0, "first"])),
            ),
            (0, "up_first"): (
                cutoff_mask,
                lambda _, got: coulomb_table(got[0, "second"][0, 0].astype(jnp.int32), count),
            ),
        },
    )
    owner = lax.axis_index("band") == owners[0]
    owned = [
        [jnp.where(owner, part, 0.0) for part in halves(orbitals[band], core == 1, 0)]
        for band in range(2)
    ]
    block = band_sum(owned, gather_band, beside, 1)
    coulomb = beside.results[0, "up_first"]
    block = [*block[0], *block[1]]
    block[0], later = tied(block[0], orbitals)
    last = across(rows_of(later, *rows[-1][1:]))
    arrived = [beside.arrived[name] for name in names] + [last]
    orbital = [(orbitals, (0, 0, 0, half)), *zip(arrived[:6], pieces(sizes[0]))]
    back_sizes = ((2, 1, 1, 1, 1), (1,) * 6)
    out_specs = [(None, 0, 0, half), *pieces(back_sizes[0])]
    *terms, own0, back0, back1, back2, back3, back4 = pair_terms(
        orbital, block, coulomb, place, tables, out_specs
    )
    back0 = across(back0)
    orbital = [(orbitals, (1, 0, 0, half)), *zip(arrived[6:], pieces(sizes[1]))]
    out_specs = [(None, 0, 0, half), *pieces(back_sizes[1])]
    results = pair_terms(orbital, block, coulomb, place, tables, out_specs, terms)
    *terms, back0 = tied(*results[:4], back0)
    own1 = results[4]
    backs = [back1, back2, back3, back4, *results[5:]]
    beside = Beside(
        {name: (back[None], 0, 0, back.shape[0]) for name, back in zip(names, backs)}
    )
    sums = band_sum([terms[:2], terms[2:]], gather_half, beside, 0)
    own_band, other_band = [joined(*parts, core == 1, 0) for parts in sums]
    block_total = jnp.stack(
        [jnp.where(plane == 1, other_band, own_band), jnp.where(plane == 1, own_band, other_band)]
    )
    arrived = [beside.arrived[name] for name in names]
    back0 = jnp.concatenate([back0] + arrived[:4], 0)
    back1 = jnp.concatenate(arrived[4:], 0)
    return jnp.stack([own0 + back0, own1 + back1]), block_total


def solution(mesh):
    in_specs = (P("band", "fft", None), P(), P(None, "fft"))
    out_specs = (P("band", "fft", None), P(None, "fft", None))

    def per_device(orbitals, owners, cutoff_mask):
        bands, rows, cells = orbitals.shape
        paired = bands == mesh.shape["fft"] == 2 and mesh.shape["band"] == 16
        paired = paired and cells % (8 * LANES) == 0 and rows % 16 == 0 and 2 * rows <= LANES
        chosen = per_device_pairs if paired else per_device_general
        return chosen(orbitals, owners, cutoff_mask)

    return jax.shard_map(
        per_device, mesh=mesh, in_specs=in_specs, out_specs=out_specs, check_vma=False
    )
```

```python
import functools
import math

import jax
import jax.numpy as jnp
import numpy as np
from jax import lax
from jax.experimental import pallas as pl
from jax.experimental.pallas import tpu as pltpu
from jax.sharding import PartitionSpec as P

COULOMB = 400.0
EXCHANGE_MIX = 0.25


def broadcast(value, axis, source):
    kept = jnp.where(lax.axis_index(axis) == source, value, 0).astype(value.dtype)
    return lax.psum(kept, axis)


def dft_tables(count):
    positions = jnp.arange(count, dtype=jnp.int32)
    phases = positions[:, None] * positions[None, :] % count
    angles = phases.astype(jnp.float32) * (2.0 * math.pi / count)
    return (jnp.cos(angles), jnp.sin(angles))


def transform_dim(values, matrix, dim):
    source = "pabc"
    target = source[:dim] + "k" + source[dim + 1 :]
    pattern = source + "," + source[dim] + "k" + "->" + target
    return jnp.einsum(pattern, values, matrix, precision=lax.Precision.HIGHEST)


def forward_local(real_data, cosine, sine):
    casine = cosine + sine
    parts = [transform_dim(transform_dim(real_data, casine, 3), casine, 2)]
    stacked = jnp.stack(parts, axis=1)
    return stacked.reshape(stacked.shape[0], stacked.shape[1], stacked.shape[2], -1)


def spectral_middle(spectrum, kernel, cosine, sine):
    count_pairs, components, grid_size, flat_cells = spectrum.shape
    shaped = spectrum.reshape(count_pairs, components, grid_size, kernel.shape[1], grid_size)
    casine = cosine + sine
    scaled = transform_dim(shaped[:, 0], casine, 1) * kernel
    parts = [transform_dim(scaled, casine, 1)]
    return jnp.stack(parts, axis=1).reshape(count_pairs, components, grid_size, flat_cells)


def inverse_local(spectrum, cosine, sine):
    count_pairs, components, slab_rows, flat_cells = spectrum.shape
    grid_size = cosine.shape[0]
    shaped = spectrum.reshape(count_pairs, components, slab_rows, grid_size, grid_size)
    casine = cosine + sine
    result = transform_dim(transform_dim(shaped[:, 0], casine, 2), casine, 3)
    result = result / float(grid_size * grid_size * grid_size)
    return result.reshape(count_pairs, slab_rows, flat_cells)


def per_device_general(orbitals, owners, cutoff_mask):
    local_bands, slab_rows, flat_cells = orbitals.shape
    grid_size = slab_rows * lax.axis_size("fft")
    cosine, sine = dft_tables(grid_size)
    positions = jnp.arange(grid_size, dtype=jnp.int32)
    signed = jnp.where(positions <= grid_size // 2, positions, positions - grid_size)
    signed_y = lax.dynamic_slice_in_dim(signed, lax.axis_index("fft") * slab_rows, slab_rows)
    squared = (
        signed[:, None, None] * signed[:, None, None]
        + signed_y[None, :, None] * signed_y[None, :, None]
        + signed[None, None, :] * signed[None, None, :]
    )
    weights = cutoff_mask.reshape(grid_size, slab_rows, grid_size).astype(jnp.float32)
    kernel = COULOMB * weights / jnp.maximum(squared, 1).astype(jnp.float32)
    local_total = jnp.zeros((local_bands, slab_rows, flat_cells), jnp.float32)
    block_orbs = broadcast(orbitals, "band", owners[0])
    pair_data = (orbitals[:, None] * block_orbs[None]).reshape(
        local_bands * local_bands, slab_rows, grid_size, grid_size
    )
    spectrum = forward_local(pair_data, cosine, sine)
    pencil_out = spectral_middle(
        lax.all_to_all(spectrum, "fft", split_axis=3, concat_axis=2, tiled=True),
        kernel,
        cosine,
        sine,
    )
    returned = lax.all_to_all(pencil_out, "fft", split_axis=2, concat_axis=3, tiled=True)
    potential = inverse_local(returned, cosine, sine).reshape(
        local_bands, local_bands, slab_rows, flat_cells
    )
    local_total = local_total - EXCHANGE_MIX * jnp.sum(block_orbs[None] * potential, axis=1)
    block_terms = -EXCHANGE_MIX * jnp.sum(orbitals[:, None] * potential, axis=0)
    block_total = lax.psum(block_terms, "band")
    return (local_total, block_total)


LANES = 128


def casine_matrix(count):
    positions = np.arange(count)
    angles = (np.outer(positions, positions) % count) * (2.0 * np.pi / count)
    return np.cos(angles) + np.sin(angles)


def split_table(matrix):
    high = matrix.astype(np.float32).astype(jnp.bfloat16)
    low = (matrix - high.astype(np.float64)).astype(np.float32).astype(jnp.bfloat16)
    return high, low


def left_table(matrix):
    high, low = split_table(matrix)
    return np.concatenate([np.concatenate([high, high], 1), np.concatenate([low, low], 1)], 0)


def right_table(matrix):
    count = matrix.shape[0]
    padded = np.zeros((LANES, LANES))
    padded[:count, :count] = matrix
    row = np.concatenate(split_table(padded), 1)
    return np.concatenate([row, row], 0)


def split(values):
    high = values.astype(jnp.bfloat16)
    return high, (values - high.astype(jnp.float32)).astype(jnp.bfloat16)


def transform_rows(table, values):
    rows = values.shape[0]
    stacked = jnp.concatenate(split(values), 0)
    result = jnp.dot(table, stacked, preferred_element_type=jnp.float32)
    return result[:rows] + result[rows:]


def transform_lanes(values, table):
    stacked = jnp.concatenate(split(values), 1)
    result = jnp.dot(stacked, table, preferred_element_type=jnp.float32)
    return result[:, :LANES] + result[:, LANES:]


def divisor(total, limit):
    return max(k for k in range(1, limit + 1) if total % k == 0)


def pair_kernel(count, unit, batch, planes, specs, has_total, place_ref, *refs):
    in_specs, out_specs = specs
    forth, along_z, *refs = refs
    half, quarter = count // 2, count // 4
    n_in = 5 + len(in_specs) + (4 if has_total else 0)
    n_out = 4 + len(out_specs)
    coulomb_in, *others = refs[:n_in]
    block_in, orbital_in, totals_in = others[:4], others[4 : 4 + len(in_specs)], others[4 + len(in_specs) :]
    terms_out, local_out = refs[n_in : n_in + 4], refs[n_in + 4 : n_in + n_out]
    first, second, coulomb, total, local, terms, cells, in_sems, out_sems, wide_sem = refs[n_in + n_out :]
    width = batch * unit
    steps = count * count // width
    plane, core = place_ref[0], place_ref[1]
    starts = (plane * half, half - plane * half)
    parts = (core * quarter, quarter - core * quarter)

    def span(ref, buffer, start, rows):
        start = start if isinstance(start, int) else pl.multiple_of(start, 8)
        return ref, buffer.at[pl.ds(start, rows)]

    def by_core(buffer, arrays):
        places = [start + part for start in starts for part in parts]
        return [span(ref, buffer, start, quarter) for ref, start in zip(arrays, places)]

    def by_spec(buffer, arrays, given):
        result = []
        for ref, (index, which, row, rows) in zip(arrays, given):
            ref = ref if index is None else ref.at[index]
            if which is None:
                result += [span(ref.at[k], buffer, k * half, half) for k in range(2)]
            else:
                result.append(span(ref, buffer, starts[which] + row, rows))
        return result

    loads = by_spec(first, orbital_in, in_specs) + by_core(second, block_in)
    late = by_core(total, totals_in) if has_total else []
    stores = by_core(terms, terms_out) + by_spec(local, local_out, out_specs)

    def copies(pairs, sems, step, offset, outward):
        columns = pl.ds(pl.multiple_of(step * width, LANES), width)
        for k, (outside, inside) in enumerate(pairs):
            ends = (outside.at[:, columns], inside.at[:, columns])
            yield pltpu.make_async_copy(*(ends[::-1] if outward else ends), sems.at[offset + k, step])

    wide = pltpu.make_async_copy(coulomb_in, coulomb, wide_sem)
    for step in range(steps):
        for copy in copies(loads, in_sems, step, 0, False):
            copy.start()
    wide.start()

    def forward(step, carry):
        for copy in copies(loads, in_sems, step, 0, False):
            copy.wait()
        columns = pl.ds(pl.multiple_of(step * width, LANES), width)
        density = transform_rows(forth[...], first[:, columns] * second[:, columns])
        pieces = []
        for start in range(0, width, unit):
            piece = density[:, start : start + unit]
            for offset in range(0, unit, count):
                shifted = pltpu.roll(piece, unit - offset, 1) if offset else piece
                pieces.append(shifted[:, :LANES])
        rows = pl.ds(pl.multiple_of(step * width, 8), width)
        cells[pl.ds(step * (width // count), width // count)] = transform_lanes(jnp.concatenate(pieces, 0), along_z[...]).reshape(width // count, count, LANES)
        return carry

    lax.fori_loop(0, steps, forward, 0)
    for step in range(steps):
        for copy in copies(late, in_sems, step, len(loads), False):
            copy.start()
    wide.wait()

    def middle(step, carry):
        start = step * planes
        cube = jnp.swapaxes(cells[:, pl.ds(pl.multiple_of(start, 8), planes), :], 0, 1)
        values = [cube[k] for k in range(planes)]
        spectrum = transform_rows(forth[...], jnp.concatenate(values, 1))
        scale = jnp.concatenate([coulomb[start + k] for k in range(planes)], 1)
        scaled = transform_rows(forth[...], spectrum * scale)
        cube = jnp.stack([scaled[:, k * LANES : (k + 1) * LANES] for k in range(planes)], 0)
        cells[:, pl.ds(pl.multiple_of(start, 8), planes), :] = jnp.swapaxes(cube, 0, 1)
        return carry

    lax.fori_loop(0, count // planes, middle, 0)
    lane = lax.broadcasted_iota(jnp.int32, (count, LANES), 1)

    def inverse(step, carry):
        rows = pl.ds(pl.multiple_of(step * width, 8), width)
        values = transform_lanes(cells[pl.ds(step * (width // count), width // count)].reshape(width, LANES), along_z[...])
        tiles = [None] * (width // LANES)

        def add(tile, value):
            tiles[tile] = value if tiles[tile] is None else tiles[tile] + value

        for start in range(0, width, count):
            tile, offset = divmod(start, LANES)
            piece = values[start : start + count]
            if offset:
                piece = pltpu.roll(piece, offset, 1)
            if offset + count <= LANES:
                add(tile, piece)
            else:
                add(tile, jnp.where(lane >= offset, piece, 0.0))
                add(tile + 1, jnp.where(lane < offset, piece, 0.0))
        potential = transform_rows(forth[...], jnp.concatenate(tiles, 1))
        for copy in copies(late, in_sems, step, len(loads), False):
            copy.wait()
        columns = pl.ds(pl.multiple_of(step * width, LANES), width)
        local[:, columns] = second[:, columns] * potential
        result = first[:, columns] * potential
        if has_total:
            result = result + total[:, columns]
        terms[:, columns] = result
        for copy in copies(stores, out_sems, step, 0, True):
            copy.start()
        return carry

    lax.fori_loop(0, steps, inverse, 0)
    for step in range(steps):
        for copy in copies(stores, out_sems, step, 0, True):
            copy.wait()


def pair_terms(orbital, block, coulomb, place, tables, out_specs, totals=()):
    arrays, in_specs = zip(*orbital)
    quarter, flat_cells = block[0].shape
    count = 4 * quarter
    unit = math.lcm(count, LANES)
    batch = divisor(flat_cells // unit, 12)
    planes = divisor(count, 32)
    steps = flat_cells // (batch * unit)
    operands = [coulomb, *block, *arrays, *totals]
    vmem = pl.BlockSpec(memory_space=pltpu.VMEM)
    anywhere = pl.BlockSpec(memory_space=pl.ANY)
    shapes = [(quarter, flat_cells)] * 4
    for _, which, _, rows in out_specs:
        shapes.append((2, 2 * quarter, flat_cells) if which is None else (rows, flat_cells))
    whole = pltpu.VMEM((count, flat_cells), jnp.float32)
    moved = 4 * sum(math.prod(s) for s in shapes + [v.shape for v in operands])
    specs = (tuple(in_specs), tuple(out_specs))
    return pl.pallas_call(
        functools.partial(pair_kernel, count, unit, batch, planes, specs, bool(totals)),
        in_specs=[pl.BlockSpec(memory_space=pltpu.SMEM)]
        + [vmem] * len(tables)
        + [anywhere] * len(operands),
        out_specs=[anywhere] * len(shapes),
        out_shape=[jax.ShapeDtypeStruct(shape, jnp.float32) for shape in shapes],
        scratch_shapes=[
            whole,
            whole,
            pltpu.VMEM(coulomb.shape, jnp.float32),
            whole if totals else pltpu.VMEM((8, LANES), jnp.float32),
            whole,
            whole,
            pltpu.VMEM((count, count, LANES), jnp.float32),
            pltpu.SemaphoreType.DMA((10 + len(in_specs), steps)),
            pltpu.SemaphoreType.DMA((6 + len(out_specs), steps)),
            pltpu.SemaphoreType.DMA,
        ],
        compiler_params=pltpu.CompilerParams(vmem_limit_bytes=52 * 2**20),
        cost_estimate=pl.CostEstimate(
            flops=6 * flat_cells * count * 16 * LANES, bytes_accessed=moved, transcendentals=0
        ),
        name="pair_terms",
    )(place, *tables, *operands)


def halves(values, upper, dim):
    size = values.shape[dim] // 2
    low = lax.slice_in_dim(values, 0, size, axis=dim)
    high = lax.slice_in_dim(values, size, 2 * size, axis=dim)
    return jnp.where(upper, high, low), jnp.where(upper, low, high)


def joined(mine, theirs, upper, dim):
    return jnp.concatenate(
        [jnp.where(upper, theirs, mine), jnp.where(upper, mine, theirs)], axis=dim
    )


def across(value):
    return lax.ppermute(value, "fft", [(0, 1), (1, 0)])


def tied(*values):
    return lax.optimization_barrier(values)


def squared_components(count):
    positions = np.arange(count)
    return np.where(positions <= count // 2, positions, positions - count).astype(np.int32) ** 2


def largest_length(cutoff_mask, count):
    squares = squared_components(count)
    flat = (squares[:, None] + squares[None, :]).reshape(-1, cutoff_mask.shape[1])
    mine = jnp.asarray(flat)[lax.axis_index("fft")]
    lengths = jnp.where(cutoff_mask != 0, squares[:, None] + mine[None, :], 0)
    return jnp.full((8, LANES), jnp.max(lengths).astype(jnp.float32))


def coulomb_table(limit, count):
    def squares(dim):
        position = lax.broadcasted_iota(jnp.int32, (count, count, LANES), dim)
        signed = jnp.where(position <= count // 2, position, position - count)
        return signed * signed

    squared = squares(0) + squares(1) + squares(2)
    weights = ((squared >= 1) & (squared <= limit)).astype(jnp.float32)
    factor = -EXCHANGE_MIX * COULOMB / float(count**3)
    return factor * weights / jnp.maximum(squared, 1).astype(jnp.float32)


def rows_of(array, index, start, rows):
    return array[index, start : start + rows]


class Beside:
    def __init__(self, sends, needed=()):
        self.sends = sends
        self.needed = dict(needed)
        self.results = {}
        self.arrived = {}

    def open(self, step, *values):
        if step in self.sends:
            array, *cut = self.sends[step]
            *values, array = tied(*values, array)
            self.arrived[step] = across(rows_of(array, *cut))
        if step in self.needed:
            array, function = self.needed[step]
            *values, array = tied(*values, array)
            self.results[step] = function(array, self.results)
        return values

    def close(self, step, value):
        for found in (self.arrived, self.results):
            if step in found:
                value, found[step] = tied(value, found[step])
        return value


def band_sum(parts, exchange, beside, flip):
    size, planes = lax.axis_size("band"), lax.axis_size("fft")
    index, plane = lax.axis_index("band"), lax.axis_index("fft")
    core, side, depth = index % 2, index // 2 % 2, index // 4
    depth_low, depth_high = (depth + depth // 2) % 2 == 1, depth // 2 == 1

    def swap(step, value, partner, kept=None):
        kept, value = beside.open(step, value if kept is None else kept, value)
        ends = [(k, f, partner(k, f)) for k in range(size) for f in range(planes)]
        pairs = [(k * planes + f, end * planes + f) for k, f, end in ends]
        arrived = lax.ppermute(value, ("band", "fft"), pairs)
        return kept, beside.close(step, arrived)

    def added(step, value, partner, kept=None):
        kept, arrived = swap(step, value, partner, kept)
        return kept + arrived

    def across_cores(k, f):
        return k ^ 1

    def axes(which, flipped):
        def by_core(first, second):
            return lambda k, f: k ^ (second if (k + which + flipped * f) % 2 else first)

        turned = (core + which + flipped * plane) % 2 == 1
        bits = jnp.where(turned, depth_low, side == 1), jnp.where(turned, depth_high, depth_low)
        return bits, (by_core(2, 4), by_core(4, 12), by_core(12, 2))

    def after(value, other):
        return value

    values = [None, None]
    earlier = [None, None]
    for which, (keep, send) in enumerate(parts):
        values[which] = added((which, "core"), send, across_cores, keep)
    for number, name in enumerate(("first", "second", "third")):
        results = []
        for which in range(2):
            bits, partners = axes(which, flip)
            value = after(values[which], earlier[1 - which])
            if number < 2:
                keep, send = halves(value, bits[number], 1)
                results.append(added((which, name), send, partners[number], keep))
            else:
                results.append(added((which, name), value, partners[number]))
        earlier, values = values, results
    values = exchange(*values)
    earlier = [None, None]
    for number, name in ((1, "up_second"), (0, "up_first")):
        results = []
        for which in range(2):
            bits, partners = axes(which, 0)
            value = after(values[which], earlier[1 - which])
            results.append(joined(*swap((which, name), value, partners[number]), bits[number], 1))
        earlier, values = values, results
    return [
        swap((which, "core_back"), after(values[which], earlier[1 - which]), across_cores)
        for which in range(2)
    ]


def per_device_pairs(orbitals, owners, cutoff_mask):
    _, half, flat_cells = orbitals.shape
    count = 2 * half
    plane = lax.axis_index("fft")
    core = lax.axis_index("band") % 2
    place = jnp.stack([plane, core]).astype(jnp.int32)
    casine = casine_matrix(count)
    tables = (jnp.asarray(left_table(casine)), jnp.asarray(right_table(casine)))
    sixth = half // 6

    def gather_band(first, second):
        mine, theirs = jnp.where(plane == 1, second, first), jnp.where(plane == 1, first, second)
        return mine, across(theirs)

    def gather_half(own, other):
        return own, across(other)

    def pieces(sizes):
        return [(None, 1, sixth * sum(sizes[:k]), sixth * size) for k, size in enumerate(sizes)]

    def sent(names, band, sizes):
        rows = pieces(sizes)
        return {(1, name): (orbitals, band, *spec[2:]) for name, spec in zip(names, rows)}

    steps = ("first", "second", "third", "up_second", "up_first")
    names = [(k, name) for name in steps for k in range(2)]
    sizes = ((1,) * 6, (1, 1, 1, 1, 2))
    rows = [(orbitals, band, *spec[2:]) for band in range(2) for spec in pieces(sizes[band])]
    beside = Beside(
        dict(zip(names, rows)),
        {
            (0, "first"): (cutoff_mask, lambda mask, got: largest_length(mask, count)),
            (0, "second"): (
                cutoff_mask,
                lambda _, got: jnp.maximum(got[0, "first"], across(got[0, "first"])),
            ),
            (0, "up_first"): (
                cutoff_mask,
                lambda _, got: coulomb_table(got[0, "second"][0, 0].astype(jnp.int32), count),
            ),
        },
    )
    owner = lax.axis_index("band") == owners[0]
    owned = [
        [jnp.where(owner, part, 0.0) for part in halves(orbitals[band], core == 1, 0)]
        for band in range(2)
    ]
    block = band_sum(owned, gather_band, beside, 1)
    coulomb = beside.results[0, "up_first"]
    block = [*block[0], *block[1]]
    block[0], later = tied(block[0], orbitals)
    last = across(rows_of(later, *rows[-1][1:]))
    arrived = [beside.arrived[name] for name in names] + [last]
    orbital = [(orbitals, (0, 0, 0, half)), *zip(arrived[:6], pieces(sizes[0]))]
    back_sizes = ((2, 1, 1, 1, 1), (1,) * 6)
    out_specs = [(None, 0, 0, half), *pieces(back_sizes[0])]
    *terms, own0, back0, back1, back2, back3, back4 = pair_terms(
        orbital, block, coulomb, place, tables, out_specs
    )
    back0 = across(back0)
    orbital = [(orbitals, (1, 0, 0, half)), *zip(arrived[6:], pieces(sizes[1]))]
    out_specs = [(None, 0, 0, half), *pieces(back_sizes[1])]
    results = pair_terms(orbital, block, coulomb, place, tables, out_specs, terms)
    *terms, back0 = tied(*results[:4], back0)
    own1 = results[4]
    backs = [back1, back2, back3, back4, *results[5:]]
    beside = Beside(
        {name: (back[None], 0, 0, back.shape[0]) for name, back in zip(names, backs)}
    )
    sums = band_sum([terms[:2], terms[2:]], gather_half, beside, 0)
    own_band, other_band = [joined(*parts, core == 1, 0) for parts in sums]
    block_total = jnp.stack(
        [jnp.where(plane == 1, other_band, own_band), jnp.where(plane == 1, own_band, other_band)]
    )
    arrived = [beside.arrived[name] for name in names]
    back0 = jnp.concatenate([back0] + arrived[:4], 0)
    back1 = jnp.concatenate(arrived[4:], 0)
    return jnp.stack([own0 + back0, own1 + back1]), block_total


def solution(mesh):
    in_specs = (P("band", "fft", None), P(), P(None, "fft"))
    out_specs = (P("band", "fft", None), P(None, "fft", None))

    def per_device(orbitals, owners, cutoff_mask):
        bands, rows, cells = orbitals.shape
        paired = bands == mesh.shape["fft"] == 2 and mesh.shape["band"] == 16
        paired = paired and cells % (8 * LANES) == 0 and rows % 16 == 0 and 2 * rows <= LANES
        chosen = per_device_pairs if paired else per_device_general
        return chosen(orbitals, owners, cutoff_mask)

    return jax.shard_map(
        per_device, mesh=mesh, in_specs=in_specs, out_specs=out_specs, check_vma=False
    )
```
